128 devices in a mesh: scen: 4 (over y_lo, core), cell: 32 (over z, x, y_hi).
Axes of the slice: x: 4, y: 4 (y_hi: 2, y_lo: 2; y = y_hi * 2 + y_lo), z: 4, core: 2. Of those that a mesh axis runs over, the one named last changes fastest.
Arguments:
- yields: bfloat16 [12, 32, 30, 131072], P(None, 'scen', None, 'cell'), may hold values from -40 to 40, as said below
- model_factor: float32 [12, 128], replicated, may hold values from 0 to 0.5
- scen_factor: float32 [32, 128], P('scen'), may hold values from 0 to 0.30618623
- year_factor: float32 [30, 128], replicated, may hold values from 0 to 0.31622776
Outputs:
- cell_factor: float32 [131072, 128], P('cell')
- column_scale: float32 [128], replicated
- cell_gram: float32 [128, 128], replicated
The draws below stay inside these ranges and needn't reach their ends.
Inputs may be any that keep to these rules, and one draw needn't show every extreme that they name: `yields`: yield anomalies; each cell has its own scale.
All inputs are finite; a program needn't handle non-finite values.
Results may differ from the reference program's by a relative error of at most 0.0057.
The reference program's roundings to bfloat16 on the way (of `khatri`) count: a program that leaves them out, or rounds other values in their place, can miss the bound.
Values sent between devices are 32-bit elements; how exact they have to be, the bound alone decides.
A program may use at most 128 MiB of HBM per device.

```python
import jax
import jax.numpy as jnp
from jax import lax

MODELS = 12
YEARS = 30
RANK = 128
CELL_DEV = 4096
SCEN = 32
CELLS = 131072


def draw_yields(key, part):
    key = jax.random.fold_in(key, 11)
    first, second = jax.random.split(key)
    levels = jax.random.uniform(first, (CELLS,), jnp.float32)
    ramp = jnp.arange(CELLS, dtype=jnp.float32) / (CELLS - 1)
    scale = 0.3 * 10.0 ** levels * 3.0 ** ramp
    noise = jnp.clip(jax.random.normal(second, (MODELS, SCEN, YEARS, CELLS), jnp.float32), -4.0, 4.0)
    return (noise * scale[None, None, None, :]).astype(jnp.bfloat16)


def block_levels(own_key, shape, shards, smallest, largest):
    loudness = 1.0
    for dim, parts in shards:
        heights = jax.random.uniform(jax.random.fold_in(jax.random.fold_in(own_key, 6), dim), (parts,), jnp.float32, smallest / len(shards), largest / len(shards))
        loudness = loudness * jnp.repeat(jnp.exp(heights), shape[dim] // parts).reshape((-1,) + (1,) * (len(shape) - 1 - dim))
    return loudness


def setup_inputs(seed: int = 0) -> dict:
    key_list = jax.random.split(jax.random.key(seed), 5)
    yields = draw_yields(jax.random.fold_in(key_list[4], 71), 0)
    model_factor = jnp.clip(jax.random.uniform(key_list[1], (MODELS, RANK), jnp.float32, 0.0, 0.5), 0.0, 0.5)
    scen_factor = jnp.clip(0.30618623 * jax.random.uniform(key_list[2], (SCEN, RANK), jnp.float32) ** block_levels(key_list[2], (SCEN, RANK), ((0, 4),), -0.2, 0.2), 0.0, 0.30618623)
    year_factor = jnp.clip(jax.random.uniform(key_list[3], (YEARS, RANK), jnp.float32, 0.0, 0.31622776), 0.0, 0.31622776)
    return {"yields": yields, "model_factor": model_factor, "scen_factor": scen_factor, "year_factor": year_factor}


ridge = 0.1
epsilon = 1e-06

def reference(yields, model_factor, scen_factor, year_factor):
    highest = lax.Precision.HIGHEST
    khatri = model_factor[:, None, None, :] * scen_factor[None, :, None, :] * year_factor[None, None, :, :]
    khatri = khatri.astype(jnp.bfloat16).reshape(-1, RANK).astype(jnp.float32)
    flat = yields.reshape(-1, CELLS)
    blocks = CELLS // CELL_DEV

    def one_block(index):
        piece = lax.dynamic_slice_in_dim(flat, index * CELL_DEV, CELL_DEV, 1).astype(jnp.float32)
        return jnp.dot(piece.T.astype(jnp.float32), khatri.astype(jnp.float32), precision=highest, preferred_element_type=jnp.float32)
    mttkrp = lax.map(one_block, jnp.arange(blocks, dtype=jnp.int32)).reshape(CELLS, RANK)
    gram_model = jnp.dot(model_factor.T, model_factor, precision=highest)
    gram_scen = jnp.dot(scen_factor.T, scen_factor, precision=highest)
    gram_year = jnp.dot(year_factor.T, year_factor, precision=highest)
    normal = gram_model * gram_scen * gram_year + ridge * jnp.eye(RANK, dtype=jnp.float32)
    raw = jnp.linalg.solve(normal, mttkrp.T).T
    column_scale = jnp.sqrt(lax.optimization_barrier(jnp.sum(raw * raw, axis=0)) / CELLS + epsilon)
    cell_factor = raw / column_scale[None, :]
    cell_gram = jnp.dot(cell_factor.T, cell_factor, precision=highest) / CELLS
    return (cell_factor, column_scale, cell_gram)
```

```python
import functools

import jax
import jax.numpy as jnp
from jax import lax
from jax.experimental import pallas as pl
from jax.experimental.pallas import tpu as pltpu
from jax.sharding import PartitionSpec as P

ridge = 0.1
epsilon = 1e-06
MESH = pl.DeviceIdType.MESH
HIGHEST = lax.Precision.HIGHEST
NT = (((1,), (1,)), ((), ()))
RANK = 128
PARTS = 4
PANEL = 16


def invert(normal, stage):
    rows = lax.broadcasted_iota(jnp.int32, (RANK, RANK), 0)
    cols = lax.broadcasted_iota(jnp.int32, (RANK, RANK), 1)
    panel_row = lax.broadcasted_iota(jnp.int32, (PANEL, RANK), 0)
    panel_col = lax.broadcasted_iota(jnp.int32, (PANEL, RANK), 1)
    a = normal
    for first in range(0, RANK, PANEL):
        panel = a[first : first + PANEL, :]
        columns = [
            jnp.broadcast_to(panel[:, first + j : first + j + 1], (PANEL, RANK))
            for j in range(PANEL)
        ]
        inside = (panel_col >= first) & (panel_col < first + PANEL)
        unit = jnp.where(panel_col - first == panel_row, 1.0, 0.0)
        right = jnp.where(inside, unit, panel)
        for k in range(PANEL):
            pivot = columns[k]
            scale = 1.0 / pivot[k : k + 1, :]
            is_pivot = panel_row == k
            top = right[k : k + 1, :] * scale
            right = jnp.where(is_pivot, top, right - pivot * top)
            for j in range(k + 1, PANEL):
                top = columns[j][k : k + 1, :] * scale
                columns[j] = jnp.where(is_pivot, top, columns[j] - pivot * top)
        parts = [right]
        if first:
            parts = [jnp.zeros((first, RANK), jnp.float32)] + parts
        if first + PANEL < RANK:
            parts = parts + [jnp.zeros((RANK - first - PANEL, RANK), jnp.float32)]
        spread = jnp.concatenate(parts, axis=0)
        in_cols = (cols >= first) & (cols < first + PANEL)
        in_rows = (rows >= first) & (rows < first + PANEL)
        update = jnp.dot(
            jnp.where(in_cols, a, 0.0), spread, precision=HIGHEST, preferred_element_type=jnp.float32
        )
        a = jnp.where(in_rows, spread, jnp.where(in_cols, 0.0, a) - update)
    return a


def gram(factor_ref, pad_ref):
    pad_ref[...] = jnp.zeros_like(pad_ref)
    pad_ref[0 : factor_ref.shape[0], :] = factor_ref[...]
    full = pad_ref[...]
    return jnp.dot(full.T, full, precision=HIGHEST, preferred_element_type=jnp.float32)


def main_kernel(
    grid_sizes, yields, model, scen, year, raw, g_out,
    ybuf, mbuf, sbuf, yearbuf, khat, kht, pad, csend, crecv, ysend, yrecv, own,
    gd, gcr, gy, gz, gx, gfin,
    yield_sems, factor_sems, send_sems, recv_sems,
):
    nz, nx = grid_sizes
    s = lax.axis_index("scen")
    c = lax.axis_index("cell")
    core = s % 2
    ylo = s // 2
    yhi = c % 2
    y = yhi * 2 + ylo
    x = (c // 2) % nx
    z = c // (2 * nx)
    quarter = yields.shape[1] // PARTS
    steps = csend.shape[0] // 2
    width = quarter // steps

    def device(core, y, z, x):
        return ((y % 2) * 2 + core, (z * nx + x) * 2 + y // 2)

    partner = device(1 - core, y, z, x)
    across = ((1 - ylo) * 2 + core, c)
    diagonal = ((1 - ylo) * 2 + 1 - core, c)
    y_peers = [device(core, (y + k) % 4, z, x) for k in (1, 2, 3)]
    z_peers = [device(core, y, (z + k) % nz, x) for k in range(1, nz)]
    x_peers = [device(core, y, z, (x + k) % nx) for k in range(1, nx)]

    counter = [0]
    sent = []

    def send(src, dst, target):
        n = counter[0]
        counter[0] += 1
        copy = pltpu.make_async_remote_copy(
            src_ref=src, dst_ref=dst, send_sem=send_sems.at[n], recv_sem=recv_sems.at[n],
            device_id=target, device_id_type=MESH,
        )
        copy.start()
        sent.append(copy)
        return copy

    q_across = (1 - ylo) * 2 + core
    q_diagonal = (1 - ylo) * 2 + 1 - core
    q_partner = ylo * 2 + 1 - core
    order = []
    for first, second in ((q_diagonal, q_across), (q_partner, s)):
        for j in range(steps):
            order += [(first, j), (second, j)]

    factor_copies = [
        pltpu.make_async_copy(src, dst, factor_sems.at[i])
        for i, (src, dst) in enumerate(((model, mbuf), (scen, sbuf.at[s]), (year, yearbuf)))
    ]
    for copy in factor_copies:
        copy.start()
    loads = []
    for i, (q, j) in enumerate(order):
        start = pl.multiple_of(q * quarter + j * width, width)
        loads.append(
            pltpu.make_async_copy(yields.at[:, pl.ds(start, width)], ybuf.at[i], yield_sems.at[i])
        )
    ahead = 4
    for copy in loads[:ahead]:
        copy.start()

    barrier = pltpu.get_barrier_semaphore()
    peers = [partner, diagonal] + y_peers + z_peers + x_peers
    for peer in peers:
        pl.semaphore_signal(barrier, inc=1, device_id=peer, device_id_type=MESH)

    for copy in factor_copies:
        copy.wait()
    local_scen = sbuf[s]
    years = yearbuf.shape[0]
    block = 8 * years
    for m in range(mbuf.shape[0]):
        ms = mbuf[m : m + 1, :] * local_scen
        khat[m * block : (m + 1) * block, :] = (ms[None, :, :] * yearbuf[...][:, None, :]).reshape(
            block, RANK
        )
    depth = khat.shape[0]
    for first in range(0, depth, RANK):
        size = min(RANK, depth - first)
        kht[:, first : first + size] = khat[first : first + size, :].T.astype(jnp.bfloat16)

    def product(i):
        loads[i].wait()
        if i + ahead < len(loads):
            loads[i + ahead].start()
        return jnp.dot(kht[...], ybuf[i], preferred_element_type=jnp.float32)

    csend[0] = product(0)
    pl.semaphore_wait(barrier, len(peers))
    scen_copies = [send(sbuf.at[s], sbuf.at[s], peer) for peer in (partner, across, diagonal)]
    to_partner = [send(csend.at[0], crecv.at[0], partner)]
    crossings = []
    for j in range(steps):
        ysend[j] = product(2 * j + 1)
        n = j + 1
        csend[n] = product(2 * n)
        to_partner.append(send(csend.at[n], crecv.at[n], partner))
        to_partner[j].wait_recv()
        ysend[j] = ysend[j] + crecv[j]
        crossings.append(send(ysend.at[j], yrecv.at[j], across))
    for j in range(steps):
        n = steps + j
        own[j] = product(2 * n + 1)
        if j + 1 < steps:
            csend[n + 1] = product(2 * n + 2)
            to_partner.append(send(csend.at[n + 1], crecv.at[n + 1], partner))

    for copy in scen_copies:
        copy.wait_recv()
    gram_model = gram(mbuf, pad)
    gram_year = gram(yearbuf, pad)
    whole_scen = sbuf[...].reshape(PARTS * sbuf.shape[1], RANK)
    pad[...] = jnp.zeros_like(pad)
    pad[0 : PARTS * sbuf.shape[1], :] = whole_scen
    full = pad[...]
    gram_scen = jnp.dot(full.T, full, precision=HIGHEST, preferred_element_type=jnp.float32)
    rows = lax.broadcasted_iota(jnp.int32, (RANK, RANK), 0)
    cols = lax.broadcasted_iota(jnp.int32, (RANK, RANK), 1)
    normal = gram_model * gram_scen * gram_year + jnp.where(rows == cols, ridge, 0.0)
    inverse = invert(normal, pad)

    def rows_of(q, j):
        return pl.ds(pl.multiple_of(q * quarter + j * width, width), width)

    gathers, late = [], []
    total = jnp.zeros((RANK, RANK), jnp.float32)
    for j in range(steps):
        to_partner[steps + j].wait_recv()
        crossings[j].wait_recv()
        summed = own[j] + crecv[steps + j] + yrecv[j]
        solved = jnp.dot(inverse, summed, precision=HIGHEST, preferred_element_type=jnp.float32)
        raw[rows_of(s, j), :] = solved.T
        here = raw.at[rows_of(s, j)]
        gathers.append(send(here, here, across))
        late.append(send(here, here, partner))
        total = total + lax.dot_general(
            solved, solved, NT, precision=HIGHEST, preferred_element_type=jnp.float32
        )

    half = RANK // 2
    gd[0] = total[0:half, :]
    gd[1] = total[half:RANK, :]
    copy = send(gd.at[1 - core], gcr, partner)
    copy.wait_recv()
    value = gd[core] + gcr[...]
    for where, slots, targets in ((y, gy, y_peers), (z, gz, z_peers), (x, gx, x_peers)):
        slots[where] = value
        copies = [send(slots.at[where], slots.at[where], target) for target in targets]
        for copy in copies:
            copy.wait_recv()
        value = slots[0]
        for k in range(1, slots.shape[0]):
            value = value + slots[k]
    gfin[core] = value
    last = send(gfin.at[core], gfin.at[core], partner)

    for j in range(steps):
        gathers[j].wait_recv()
        here = raw.at[rows_of(q_across, j)]
        late.append(send(here, here, partner))
    last.wait_recv()
    g_out[...] = gfin[...].reshape(RANK, RANK)
    for copy in sent:
        copy.wait_send()
    for copy in late:
        copy.wait_recv()


def finish_kernel(cells, raw, g, factor, scale, cell_gram):
    rows = lax.broadcasted_iota(jnp.int32, (RANK, RANK), 0)
    cols = lax.broadcasted_iota(jnp.int32, (RANK, RANK), 1)
    products = g[...]
    diagonal = jnp.where(rows == cols, products, 0.0)
    along = jnp.sqrt(jnp.sum(diagonal, axis=0, keepdims=True) / cells + epsilon)
    down = jnp.sqrt(jnp.sum(diagonal, axis=1, keepdims=True) / cells + epsilon)
    scale[...] = along
    inverse = 1.0 / along
    cell_gram[...] = products * inverse * (1.0 / down) / cells
    factor[...] = raw[...] * inverse


def on_device(grid_sizes, yields, model_factor, scen_factor, year_factor):
    models, scens, years, local_cells = yields.shape
    rank = model_factor.shape[1]
    total_cells = local_cells * lax.axis_size("cell")
    flat = yields.transpose(0, 2, 1, 3).reshape(-1, local_cells)
    depth = flat.shape[0]
    quarter = local_cells // PARTS
    width = 256
    steps = quarter // width
    f32 = jnp.float32
    any_space = pl.BlockSpec(memory_space=pl.ANY)
    vmem = pl.BlockSpec(memory_space=pltpu.VMEM)
    copies = 80
    raw, products = pl.pallas_call(
        functools.partial(main_kernel, grid_sizes),
        out_shape=(
            jax.ShapeDtypeStruct((local_cells, rank), f32),
            jax.ShapeDtypeStruct((rank, rank), f32),
        ),
        in_specs=[any_space] * 4,
        out_specs=(vmem, vmem),
        scratch_shapes=[
            pltpu.VMEM((4 * steps, depth, width), jnp.bfloat16),
            pltpu.VMEM((models, rank), f32),
            pltpu.VMEM((PARTS, scens, rank), f32),
            pltpu.VMEM((years, rank), f32),
            pltpu.VMEM((depth, rank), f32),
            pltpu.VMEM((rank, depth), jnp.bfloat16),
            pltpu.VMEM((rank, rank), f32),
            pltpu.VMEM((2 * steps, rank, width), f32),
            pltpu.VMEM((2 * steps, rank, width), f32),
            pltpu.VMEM((steps, rank, width), f32),
            pltpu.VMEM((steps, rank, width), f32),
            pltpu.VMEM((steps, rank, width), f32),
            pltpu.VMEM((2, rank // 2, rank), f32),
            pltpu.VMEM((rank // 2, rank), f32),
            pltpu.VMEM((4, rank // 2, rank), f32),
            pltpu.VMEM((grid_sizes[0], rank // 2, rank), f32),
            pltpu.VMEM((grid_sizes[1], rank // 2, rank), f32),
            pltpu.VMEM((2, rank // 2, rank), f32),
            pltpu.SemaphoreType.DMA((4 * steps,)),
            pltpu.SemaphoreType.DMA((3,)),
            pltpu.SemaphoreType.DMA((copies,)),
            pltpu.SemaphoreType.DMA((copies,)),
        ],
        compiler_params=pltpu.CompilerParams(
            collective_id=0, has_side_effects=True, vmem_limit_bytes=52 << 20
        ),
    )(flat, model_factor, scen_factor, year_factor)
    cell_factor, column_scale, cell_gram = pl.pallas_call(
        functools.partial(finish_kernel, float(total_cells)),
        out_shape=(
            jax.ShapeDtypeStruct((local_cells, rank), f32),
            jax.ShapeDtypeStruct((1, rank), f32),
            jax.ShapeDtypeStruct((rank, rank), f32),
        ),
        in_specs=[vmem, vmem],
        out_specs=(vmem, vmem, vmem),
    )(raw, products)
    return cell_factor, column_scale.reshape(rank), cell_gram


def solution(mesh):
    cells = mesh.shape["cell"]
    grid_sizes = (4, cells // 8)
    in_specs = (P(None, "scen", None, "cell"), P(), P("scen", None), P())
    out_specs = (P("cell", None), P(), P())
    return jax.shard_map(
        functools.partial(on_device, grid_sizes), mesh=mesh, in_specs=in_specs, out_specs=out_specs, check_vma=False
    )
```

```python
import functools

import jax
import jax.numpy as jnp
from jax import lax
from jax.experimental import pallas as pl
from jax.experimental.pallas import tpu as pltpu
from jax.sharding import PartitionSpec as P

ridge = 0.1
epsilon = 1e-06
MESH = pl.DeviceIdType.MESH
HIGHEST = lax.Precision.HIGHEST
NT = (((1,), (1,)), ((), ()))
RANK = 128
PARTS = 4
PANEL = 16
WIDTHS = (128, 256, 256, 256, 128)


def invert(normal, stage):
    rows = lax.broadcasted_iota(jnp.int32, (RANK, RANK), 0)
    cols = lax.broadcasted_iota(jnp.int32, (RANK, RANK), 1)
    panel_row = lax.broadcasted_iota(jnp.int32, (PANEL, RANK), 0)
    panel_col = lax.broadcasted_iota(jnp.int32, (PANEL, RANK), 1)
    a = normal
    for first in range(0, RANK, PANEL):
        panel = a[first : first + PANEL, :]
        columns = [
            jnp.broadcast_to(panel[:, first + j : first + j + 1], (PANEL, RANK))
            for j in range(PANEL)
        ]
        inside = (panel_col >= first) & (panel_col < first + PANEL)
        unit = jnp.where(panel_col - first == panel_row, 1.0, 0.0)
        right = jnp.where(inside, unit, panel)
        for k in range(PANEL):
            pivot = columns[k]
            scale = 1.0 / pivot[k : k + 1, :]
            is_pivot = panel_row == k
            top = right[k : k + 1, :] * scale
            right = jnp.where(is_pivot, top, right - pivot * top)
            for j in range(k + 1, PANEL):
                top = columns[j][k : k + 1, :] * scale
                columns[j] = jnp.where(is_pivot, top, columns[j] - pivot * top)
        parts = [right]
        if first:
            parts = [jnp.zeros((first, RANK), jnp.float32)] + parts
        if first + PANEL < RANK:
            parts = parts + [jnp.zeros((RANK - first - PANEL, RANK), jnp.float32)]
        spread = jnp.concatenate(parts, axis=0)
        in_cols = (cols >= first) & (cols < first + PANEL)
        in_rows = (rows >= first) & (rows < first + PANEL)
        update = jnp.dot(
            jnp.where(in_cols, a, 0.0), spread, precision=HIGHEST, preferred_element_type=jnp.float32
        )
        a = jnp.where(in_rows, spread, jnp.where(in_cols, 0.0, a) - update)
    return a


def gram(factor_ref, pad_ref):
    pad_ref[...] = jnp.zeros_like(pad_ref)
    pad_ref[0 : factor_ref.shape[0], :] = factor_ref[...]
    full = pad_ref[...]
    return jnp.dot(full.T, full, precision=HIGHEST, preferred_element_type=jnp.float32)


def main_kernel(
    grid_sizes, widths, yields, model, scen, year, raw, g_out,
    ybufs, mbuf, sbuf, yearbuf, khat, kht, pad, csend, crecv, ysend, yrecv, own,
    gd, gcr, gy, gz, gx, gfin,
    yield_sems, factor_sems, send_sems, recv_sems,
):
    nz, nx = grid_sizes
    s = lax.axis_index("scen")
    c = lax.axis_index("cell")
    core = s % 2
    ylo = s // 2
    yhi = c % 2
    y = yhi * 2 + ylo
    x = (c // 2) % nx
    z = c // (2 * nx)
    quarter = yields.shape[1] // PARTS
    steps = len(widths)
    offsets = [sum(widths[:j]) for j in range(steps)]

    def device(core, y, z, x):
        return ((y % 2) * 2 + core, (z * nx + x) * 2 + y // 2)

    partner = device(1 - core, y, z, x)
    across = ((1 - ylo) * 2 + core, c)
    diagonal = ((1 - ylo) * 2 + 1 - core, c)
    y_peers = [device(core, (y + k) % 4, z, x) for k in (2, 1, 3)]
    z_peers = [device(core, y, (z + k) % nz, x) for k in (2, 1, 3)]
    x_peers = [device(core, y, z, (x + k) % nx) for k in (2, 1, 3)]
    first_slot = z * (1 - core) + x * core
    second_slot = x * (1 - core) + z * core
    first_peers = [
        device(core, y, (z + k * (1 - core)) % nz, (x + k * core) % nx) for k in (2, 1, 3)
    ]
    second_peers = [
        device(core, y, (z + k * core) % nz, (x + k * (1 - core)) % nx) for k in (2, 1, 3)
    ]

    sent = []
    received = set()

    def send(src, dst, target):
        n = len(sent)
        copy = pltpu.make_async_remote_copy(
            src_ref=src, dst_ref=dst, send_sem=send_sems.at[n], recv_sem=recv_sems.at[n],
            device_id=target, device_id_type=MESH,
        )
        copy.start()
        sent.append(copy)
        return n

    left = set()

    def leave(n):
        left.add(n)
        sent[n].wait_send()

    def arrive(n):
        received.add(n)
        sent[n].wait_recv()

    q_across = (1 - ylo) * 2 + core
    q_diagonal = (1 - ylo) * 2 + 1 - core
    q_partner = ylo * 2 + 1 - core
    order = []
    for first, second in ((q_diagonal, q_across), (q_partner, s)):
        for j in range(steps):
            order += [(first, j), (second, j)]

    factor_copies = [
        pltpu.make_async_copy(src, dst, factor_sems.at[i])
        for i, (src, dst) in enumerate(((model, mbuf), (scen, sbuf.at[s]), (year, yearbuf)))
    ]
    for copy in factor_copies:
        copy.start()

    def columns(q, j):
        return pl.ds(pl.multiple_of(q * quarter + offsets[j], 128), widths[j])

    loads = []
    for i, (q, j) in enumerate(order):
        slot = ybufs.at[i, :, pl.ds(0, widths[j])]
        loads.append(pltpu.make_async_copy(yields.at[:, columns(q, j)], slot, yield_sems.at[i]))
    ahead = [0]

    def load_until(n):
        for copy in loads[ahead[0] : n]:
            copy.start()
        ahead[0] = max(ahead[0], min(n, len(loads)))

    load_until(3)
    barrier = pltpu.get_barrier_semaphore()
    peers = [partner, diagonal] + y_peers + z_peers + x_peers
    for peer in peers:
        pl.semaphore_signal(barrier, inc=1, device_id=peer, device_id_type=MESH)

    for copy in factor_copies:
        copy.wait()
    local_scen = sbuf[s]
    years = yearbuf.shape[0]
    block = 8 * years
    for m in range(mbuf.shape[0]):
        ms = mbuf[m : m + 1, :] * local_scen
        khat[m * block : (m + 1) * block, :] = (ms[None, :, :] * yearbuf[...][:, None, :]).reshape(
            block, RANK
        )
    depth = khat.shape[0]
    for first in range(0, depth, RANK):
        size = min(RANK, depth - first)
        kht[:, first : first + size] = khat[first : first + size, :].T.astype(jnp.bfloat16)

    def product(i):
        loads[i].wait()
        load_until(i + 6)
        return jnp.dot(
            kht[...], ybufs[i, :, 0 : widths[order[i][1]]], preferred_element_type=jnp.float32
        )

    def part(ref, n):
        return ref.at[n, :, pl.ds(0, widths[n % steps])]

    part(csend, 0)[...] = product(0)
    pl.semaphore_wait(barrier, len(peers))
    to_partner = [send(part(csend, 0), part(crecv, 0), partner)]
    scen_copies = []
    crossings = []
    gathers = []
    late = []

    def rows_of(q, j):
        return pl.ds(pl.multiple_of(q * quarter + offsets[j], 128), widths[j])

    for j in range(steps):
        part(ysend, j)[...] = product(2 * j + 1)
        n = j + 1
        part(csend, n)[...] = product(2 * n)
        to_partner.append(send(part(csend, n), part(crecv, n), partner))
        arrive(to_partner[j])
        part(ysend, j)[...] = part(ysend, j)[...] + part(crecv, j)[...]
        crossings.append(send(part(ysend, j), part(yrecv, j), across))
        if j == 0:
            scen_copies = [
                send(sbuf.at[s], sbuf.at[s], peer) for peer in (across, diagonal, partner)
            ]
    for j in range(steps):
        n = steps + j
        part(own, j)[...] = product(2 * n + 1)
        if j + 1 < steps:
            part(csend, n + 1)[...] = product(2 * n + 2)
            to_partner.append(send(part(csend, n + 1), part(crecv, n + 1), partner))

    for n in scen_copies:
        arrive(n)
    gram_model = gram(mbuf, pad)
    gram_year = gram(yearbuf, pad)
    whole_scen = sbuf[...].reshape(PARTS * sbuf.shape[1], RANK)
    pad[...] = jnp.zeros_like(pad)
    pad[0 : PARTS * sbuf.shape[1], :] = whole_scen
    full = pad[...]
    gram_scen = jnp.dot(full.T, full, precision=HIGHEST, preferred_element_type=jnp.float32)
    rows = lax.broadcasted_iota(jnp.int32, (RANK, RANK), 0)
    cols = lax.broadcasted_iota(jnp.int32, (RANK, RANK), 1)
    normal = gram_model * gram_scen * gram_year + jnp.where(rows == cols, ridge, 0.0)
    inverse = invert(normal, pad)

    total = jnp.zeros((RANK, RANK), jnp.float32)

    def keep(j, solved):
        raw[rows_of(s, j), :] = solved.T
        here = raw.at[rows_of(s, j)]
        gathers.append(send(here, here, across))
        late.append(send(here, here, partner))

    for j in range(steps):
        arrive(to_partner[steps + j])
        arrive(crossings[j])
        summed = part(own, j)[...] + part(crecv, steps + j)[...] + part(yrecv, j)[...]
        solved = jnp.dot(inverse, summed, precision=HIGHEST, preferred_element_type=jnp.float32)
        total = total + lax.dot_general(
            solved, solved, NT, precision=HIGHEST, preferred_element_type=jnp.float32
        )
        if j + 1 < steps:
            keep(j, solved)

    half = RANK // 2
    gd[0] = total[0:half, :]
    gd[1] = total[half:RANK, :]
    halves = send(gd.at[1 - core], gcr, partner)
    keep(steps - 1, solved)
    arrive(halves)
    value = gd[core] + gcr[...]
    for phase, (where, slots, targets) in enumerate(
        ((first_slot, gz, first_peers), (second_slot, gx, second_peers), (y, gy, y_peers))
    ):
        slots[where] = value
        done = list(sent)
        copies = [send(slots.at[where], slots.at[where], target) for target in targets]
        if phase == 2:
            for j in range(steps):
                arrive(gathers[j])
                here = raw.at[rows_of(q_across, j)]
                late.append(send(here, here, partner))
        for n, copy in enumerate(done):
            if n not in left and (phase == 2 or n not in gathers):
                leave(n)
        for n in copies:
            arrive(n)
        value = slots[0]
        for k in range(1, slots.shape[0]):
            value = value + slots[k]
    gfin[core] = value
    last = send(gfin.at[core], gfin.at[core], partner)
    for n in range(len(sent)):
        if n != last:
            if n not in left:
                leave(n)
            if n not in received:
                arrive(n)
    arrive(last)
    g_out[...] = gfin[...].reshape(RANK, RANK)
    leave(last)


def finish_kernel(cells, raw, g, factor, scale, cell_gram, scaled, small, grams, sems):
    rows = lax.broadcasted_iota(jnp.int32, (RANK, RANK), 0)
    cols = lax.broadcasted_iota(jnp.int32, (RANK, RANK), 1)
    products = g[...]
    diagonal = jnp.where(rows == cols, products, 0.0)
    along = jnp.sqrt(jnp.sum(diagonal, axis=0, keepdims=True) / cells + epsilon)
    inverse = 1.0 / along
    copies = []
    count = sems.shape[0] - 2
    rows_each = raw.shape[0] // count
    for i in range(count):
        here = pl.ds(i * rows_each, rows_each)
        scaled[here, :] = raw[here, :] * inverse
        copies.append(pltpu.make_async_copy(scaled.at[here], factor.at[here], sems.at[i]))
        copies[-1].start()
    down = jnp.sqrt(jnp.sum(diagonal, axis=1, keepdims=True) / cells + epsilon)
    small[...] = along
    grams[...] = products * inverse * (1.0 / down) / cells
    copies.append(pltpu.make_async_copy(small, scale, sems.at[count]))
    copies.append(pltpu.make_async_copy(grams, cell_gram, sems.at[count + 1]))
    copies[-1].start()
    copies[-2].start()
    for copy in copies:
        copy.wait()


def on_device(grid_sizes, yields, model_factor, scen_factor, year_factor):
    models, scens, years, local_cells = yields.shape
    rank = model_factor.shape[1]
    total_cells = local_cells * lax.axis_size("cell")
    flat = yields.transpose(0, 2, 1, 3).reshape(-1, local_cells)
    depth = flat.shape[0]
    steps = len(WIDTHS)
    width = max(WIDTHS)
    f32 = jnp.float32
    hbm = pl.BlockSpec(memory_space=pltpu.HBM)
    vmem = pl.BlockSpec(memory_space=pltpu.VMEM)
    copies = 64
    operands = [
        pltpu.with_memory_space_constraint(array, pltpu.HBM)
        for array in (flat, model_factor, scen_factor, year_factor)
    ]
    raw, products = pl.pallas_call(
        functools.partial(main_kernel, grid_sizes, WIDTHS),
        out_shape=(
            pltpu.VMEM((local_cells, rank), f32),
            pltpu.VMEM((rank, rank), f32),
        ),
        in_specs=[hbm] * 4,
        out_specs=(vmem, vmem),
        scratch_shapes=[
            pltpu.VMEM((4 * steps, depth, width), jnp.bfloat16),
            pltpu.VMEM((models, rank), f32),
            pltpu.VMEM((PARTS, scens, rank), f32),
            pltpu.VMEM((years, rank), f32),
            pltpu.VMEM((depth, rank), f32),
            pltpu.VMEM((rank, depth), jnp.bfloat16),
            pltpu.VMEM((rank, rank), f32),
            pltpu.VMEM((2 * steps, rank, width), f32),
            pltpu.VMEM((2 * steps, rank, width), f32),
            pltpu.VMEM((steps, rank, width), f32),
            pltpu.VMEM((steps, rank, width), f32),
            pltpu.VMEM((steps, rank, width), f32),
            pltpu.VMEM((2, rank // 2, rank), f32),
            pltpu.VMEM((rank // 2, rank), f32),
            pltpu.VMEM((4, rank // 2, rank), f32),
            pltpu.VMEM((grid_sizes[0], rank // 2, rank), f32),
            pltpu.VMEM((grid_sizes[1], rank // 2, rank), f32),
            pltpu.VMEM((2, rank // 2, rank), f32),
            pltpu.SemaphoreType.DMA((4 * steps,)),
            pltpu.SemaphoreType.DMA((3,)),
            pltpu.SemaphoreType.DMA((copies,)),
            pltpu.SemaphoreType.DMA((copies,)),
        ],
        compiler_params=pltpu.CompilerParams(
            collective_id=0, has_side_effects=True, vmem_limit_bytes=48 << 20
        ),
    )(*operands)
    cell_factor, column_scale, cell_gram = pl.pallas_call(
        functools.partial(finish_kernel, float(total_cells)),
        out_shape=(
            jax.ShapeDtypeStruct((local_cells, rank), f32),
            jax.ShapeDtypeStruct((1, rank), f32),
            jax.ShapeDtypeStruct((rank, rank), f32),
        ),
        in_specs=[vmem, vmem],
        out_specs=(hbm, hbm, hbm),
        scratch_shapes=[
            pltpu.VMEM((local_cells, rank), f32),
            pltpu.VMEM((1, rank), f32),
            pltpu.VMEM((rank, rank), f32),
            pltpu.SemaphoreType.DMA((10,)),
        ],
        compiler_params=pltpu.CompilerParams(vmem_limit_bytes=16 << 20),
    )(raw, products)
    return cell_factor, column_scale.reshape(rank), cell_gram


def solution(mesh):
    cells = mesh.shape["cell"]
    grid_sizes = (4, cells // 8)
    in_specs = (P(None, "scen", None, "cell"), P(), P("scen", None), P())
    out_specs = (P("cell", None), P(), P())
    return jax.shard_map(
        functools.partial(on_device, grid_sizes), mesh=mesh, in_specs=in_specs, out_specs=out_specs, check_vma=False
    )
```

```python
import functools

import jax
import jax.numpy as jnp
from jax import lax
from jax.experimental import pallas as pl
from jax.experimental.pallas import tpu as pltpu
from jax.sharding import PartitionSpec as P

ridge = 0.1
epsilon = 1e-06
MESH = pl.DeviceIdType.MESH
HIGHEST = lax.Precision.HIGHEST
NT = (((1,), (1,)), ((), ()))
RANK = 128
PARTS = 4
PANEL = 16
WIDTHS = (128, 384, 384, 128)


def invert(normal, stage):
    rows = lax.broadcasted_iota(jnp.int32, (RANK, RANK), 0)
    cols = lax.broadcasted_iota(jnp.int32, (RANK, RANK), 1)
    panel_row = lax.broadcasted_iota(jnp.int32, (PANEL, RANK), 0)
    panel_col = lax.broadcasted_iota(jnp.int32, (PANEL, RANK), 1)
    a = normal
    for first in range(0, RANK, PANEL):
        panel = a[first : first + PANEL, :]
        columns = [
            jnp.broadcast_to(panel[:, first + j : first + j + 1], (PANEL, RANK))
            for j in range(PANEL)
        ]
        inside = (panel_col >= first) & (panel_col < first + PANEL)
        unit = jnp.where(panel_col - first == panel_row, 1.0, 0.0)
        right = jnp.where(inside, unit, panel)
        for k in range(PANEL):
            pivot = columns[k]
            scale = 1.0 / pivot[k : k + 1, :]
            is_pivot = panel_row == k
            top = right[k : k + 1, :] * scale
            right = jnp.where(is_pivot, top, right - pivot * top)
            for j in range(k + 1, PANEL):
                top = columns[j][k : k + 1, :] * scale
                columns[j] = jnp.where(is_pivot, top, columns[j] - pivot * top)
        parts = [right]
        if first:
            parts = [jnp.zeros((first, RANK), jnp.float32)] + parts
        if first + PANEL < RANK:
            parts = parts + [jnp.zeros((RANK - first - PANEL, RANK), jnp.float32)]
        spread = jnp.concatenate(parts, axis=0)
        in_cols = (cols >= first) & (cols < first + PANEL)
        in_rows = (rows >= first) & (rows < first + PANEL)
        update = jnp.dot(
            jnp.where(in_cols, a, 0.0), spread, precision=HIGHEST, preferred_element_type=jnp.float32
        )
        a = jnp.where(in_rows, spread, jnp.where(in_cols, 0.0, a) - update)
    return a


def gram(factor_ref, pad_ref):
    pad_ref[...] = jnp.zeros_like(pad_ref)
    pad_ref[0 : factor_ref.shape[0], :] = factor_ref[...]
    full = pad_ref[...]
    return jnp.dot(full.T, full, precision=HIGHEST, preferred_element_type=jnp.float32)


def main_kernel(
    grid_sizes, widths, yields, model, scen, year, raw, g_out,
    ybufs, mbuf, sbuf, yearbuf, khat, kht, pad, csend, crecv, ysend, yrecv, own,
    gd, gcr, gy, gz, gx, gfin,
    yield_sems, factor_sems, send_sems, recv_sems,
):
    nz, nx = grid_sizes
    s = lax.axis_index("scen")
    c = lax.axis_index("cell")
    core = s % 2
    ylo = s // 2
    yhi = c % 2
    y = yhi * 2 + ylo
    x = (c // 2) % nx
    z = c // (2 * nx)
    quarter = yields.shape[1] // PARTS
    steps = len(widths)
    offsets = [sum(widths[:j]) for j in range(steps)]

    def device(core, y, z, x):
        return ((y % 2) * 2 + core, (z * nx + x) * 2 + y // 2)

    partner = device(1 - core, y, z, x)
    across = ((1 - ylo) * 2 + core, c)
    diagonal = ((1 - ylo) * 2 + 1 - core, c)
    y_peers = [device(core, (y + k) % 4, z, x) for k in (2, 1, 3)]
    z_peers = [device(core, y, (z + k) % nz, x) for k in (2, 1, 3)]
    x_peers = [device(core, y, z, (x + k) % nx) for k in (2, 1, 3)]
    first_slot = z * (1 - core) + x * core
    second_slot = x * (1 - core) + z * core
    first_peers = [
        device(core, y, (z + k * (1 - core)) % nz, (x + k * core) % nx) for k in (2, 1, 3)
    ]
    second_peers = [
        device(core, y, (z + k * core) % nz, (x + k * (1 - core)) % nx) for k in (2, 1, 3)
    ]

    sent = []
    received = set()

    def send(src, dst, target):
        n = len(sent)
        copy = pltpu.make_async_remote_copy(
            src_ref=src, dst_ref=dst, send_sem=send_sems.at[n], recv_sem=recv_sems.at[n],
            device_id=target, device_id_type=MESH,
        )
        copy.start()
        sent.append(copy)
        return n

    left = set()

    def leave(n):
        left.add(n)
        sent[n].wait_send()

    def arrive(n):
        received.add(n)
        sent[n].wait_recv()

    q_across = (1 - ylo) * 2 + core
    q_diagonal = (1 - ylo) * 2 + 1 - core
    q_partner = ylo * 2 + 1 - core
    order = []
    for first, second in ((q_diagonal, q_across), (q_partner, s)):
        for j in range(steps):
            order += [(first, j), (second, j)]

    factor_copies = [
        pltpu.make_async_copy(src, dst, factor_sems.at[i])
        for i, (src, dst) in enumerate(((model, mbuf), (scen, sbuf.at[s]), (year, yearbuf)))
    ]
    for copy in factor_copies:
        copy.start()

    def columns(q, j):
        return pl.ds(pl.multiple_of(q * quarter + offsets[j], 128), widths[j])

    loads = []
    for i, (q, j) in enumerate(order):
        slot = ybufs.at[i, :, pl.ds(0, widths[j])]
        loads.append(pltpu.make_async_copy(yields.at[:, columns(q, j)], slot, yield_sems.at[i]))
    ahead = [0]

    def load_until(n):
        for copy in loads[ahead[0] : n]:
            copy.start()
        ahead[0] = max(ahead[0], min(n, len(loads)))

    load_until(2)
    barrier = pltpu.get_barrier_semaphore()
    peers = [partner, diagonal] + y_peers + z_peers + x_peers
    for peer in peers:
        pl.semaphore_signal(barrier, inc=1, device_id=peer, device_id_type=MESH)

    for copy in factor_copies:
        copy.wait()
    local_scen = sbuf[s]
    years = yearbuf.shape[0]
    block = 8 * years
    for m in range(mbuf.shape[0]):
        ms = mbuf[m : m + 1, :] * local_scen
        khat[m * block : (m + 1) * block, :] = (ms[None, :, :] * yearbuf[...][:, None, :]).reshape(
            block, RANK
        )
    depth = khat.shape[0]
    for first in range(0, depth, RANK):
        size = min(RANK, depth - first)
        kht[:, first : first + size] = khat[first : first + size, :].T.astype(jnp.bfloat16)

    def product(i):
        loads[i].wait()
        load_until(i + 6)
        return jnp.dot(
            kht[...], ybufs[i, :, 0 : widths[order[i][1]]], preferred_element_type=jnp.float32
        )

    def part(ref, n):
        return ref.at[n, :, pl.ds(0, widths[n % steps])]

    part(csend, 0)[...] = product(0)
    pl.semaphore_wait(barrier, len(peers))
    to_partner = [send(part(csend, 0), part(crecv, 0), partner)]
    scen_copies = []
    crossings = []
    gathers = []
    late = []

    def rows_of(q, j):
        return pl.ds(pl.multiple_of(q * quarter + offsets[j], 128), widths[j])

    for j in range(steps):
        part(ysend, j)[...] = product(2 * j + 1)
        n = j + 1
        if j:
            part(csend, n)[...] = product(2 * n)
            to_partner.append(send(part(csend, n), part(crecv, n), partner))
        arrive(to_partner[j])
        part(ysend, j)[...] = part(ysend, j)[...] + part(crecv, j)[...]
        crossings.append(send(part(ysend, j), part(yrecv, j), across))
        if j == 0:
            scen_copies = [
                send(sbuf.at[s], sbuf.at[s], peer) for peer in (across, diagonal, partner)
            ]
            part(csend, n)[...] = product(2 * n)
            to_partner.append(send(part(csend, n), part(crecv, n), partner))
    for j in range(steps):
        n = steps + j
        part(own, j)[...] = product(2 * n + 1)
        if j + 1 < steps:
            part(csend, n + 1)[...] = product(2 * n + 2)
            to_partner.append(send(part(csend, n + 1), part(crecv, n + 1), partner))

    for n in scen_copies:
        arrive(n)
    gram_model = gram(mbuf, pad)
    gram_year = gram(yearbuf, pad)
    whole_scen = sbuf[...].reshape(PARTS * sbuf.shape[1], RANK)
    pad[...] = jnp.zeros_like(pad)
    pad[0 : PARTS * sbuf.shape[1], :] = whole_scen
    full = pad[...]
    gram_scen = jnp.dot(full.T, full, precision=HIGHEST, preferred_element_type=jnp.float32)
    rows = lax.broadcasted_iota(jnp.int32, (RANK, RANK), 0)
    cols = lax.broadcasted_iota(jnp.int32, (RANK, RANK), 1)
    normal = gram_model * gram_scen * gram_year + jnp.where(rows == cols, ridge, 0.0)
    inverse = invert(normal, pad)

    total = jnp.zeros((RANK, RANK), jnp.float32)

    def keep(j, solved):
        raw[rows_of(s, j), :] = solved.T
        here = raw.at[rows_of(s, j)]
        gathers.append(send(here, here, across))
        late.append(send(here, here, partner))

    for j in range(steps):
        arrive(to_partner[steps + j])
        arrive(crossings[j])
        summed = part(own, j)[...] + part(crecv, steps + j)[...] + part(yrecv, j)[...]
        solved = jnp.dot(inverse, summed, precision=HIGHEST, preferred_element_type=jnp.float32)
        total = total + lax.dot_general(
            solved, solved, NT, precision=HIGHEST, preferred_element_type=jnp.float32
        )
        if j + 1 < steps:
            keep(j, solved)

    half = RANK // 2
    gd[0] = total[0:half, :]
    gd[1] = total[half:RANK, :]
    halves = send(gd.at[1 - core], gcr, partner)
    keep(steps - 1, solved)
    arrive(halves)
    value = gd[core] + gcr[...]
    for phase, (where, slots, targets) in enumerate(
        ((first_slot, gz, first_peers), (second_slot, gx, second_peers), (y, gy, y_peers))
    ):
        slots[where] = value
        done = list(sent)
        copies = [send(slots.at[where], slots.at[where], target) for target in targets]
        if phase == 2:
            for j in range(steps):
                arrive(gathers[j])
                here = raw.at[rows_of(q_across, j)]
                late.append(send(here, here, partner))
        for n, copy in enumerate(done):
            if n not in left and (phase == 2 or n not in gathers):
                leave(n)
        for n in copies:
            arrive(n)
        value = slots[0]
        for k in range(1, slots.shape[0]):
            value = value + slots[k]
    gfin[core] = value
    last = send(gfin.at[core], gfin.at[core], partner)
    for n in range(len(sent)):
        if n != last:
            if n not in left:
                leave(n)
            if n not in received:
                arrive(n)
    arrive(last)
    g_out[...] = gfin[...].reshape(RANK, RANK)
    leave(last)


def finish_kernel(cells, raw, g, factor, scale, cell_gram, scaled, small, grams, sems):
    rows = lax.broadcasted_iota(jnp.int32, (RANK, RANK), 0)
    cols = lax.broadcasted_iota(jnp.int32, (RANK, RANK), 1)
    products = g[...]
    diagonal = jnp.where(rows == cols, products, 0.0)
    along = jnp.sqrt(jnp.sum(diagonal, axis=0, keepdims=True) / cells + epsilon)
    inverse = 1.0 / along
    copies = []
    count = sems.shape[0] - 2
    rows_each = raw.shape[0] // count
    for i in range(count):
        here = pl.ds(i * rows_each, rows_each)
        scaled[here, :] = raw[here, :] * inverse
        copies.append(pltpu.make_async_copy(scaled.at[here], factor.at[here], sems.at[i]))
        copies[-1].start()
    down = jnp.sqrt(jnp.sum(diagonal, axis=1, keepdims=True) / cells + epsilon)
    small[...] = along
    grams[...] = products * inverse * (1.0 / down) / cells
    copies.append(pltpu.make_async_copy(small, scale, sems.at[count]))
    copies.append(pltpu.make_async_copy(grams, cell_gram, sems.at[count + 1]))
    copies[-1].start()
    copies[-2].start()
    for copy in copies:
        copy.wait()


def on_device(grid_sizes, yields, model_factor, scen_factor, year_factor):
    models, scens, years, local_cells = yields.shape
    rank = model_factor.shape[1]
    total_cells = local_cells * lax.axis_size("cell")
    flat = yields.transpose(0, 2, 1, 3).reshape(-1, local_cells)
    depth = flat.shape[0]
    steps = len(WIDTHS)
    width = max(WIDTHS)
    f32 = jnp.float32
    hbm = pl.BlockSpec(memory_space=pltpu.HBM)
    vmem = pl.BlockSpec(memory_space=pltpu.VMEM)
    copies = 64
    operands = [
        pltpu.with_memory_space_constraint(array, pltpu.HBM)
        for array in (flat, model_factor, scen_factor, year_factor)
    ]
    raw, products = pl.pallas_call(
        functools.partial(main_kernel, grid_sizes, WIDTHS),
        out_shape=(
            pltpu.VMEM((local_cells, rank), f32),
            pltpu.VMEM((rank, rank), f32),
        ),
        in_specs=[hbm] * 4,
        out_specs=(vmem, vmem),
        scratch_shapes=[
            pltpu.VMEM((4 * steps, depth, width), jnp.bfloat16),
            pltpu.VMEM((models, rank), f32),
            pltpu.VMEM((PARTS, scens, rank), f32),
            pltpu.VMEM((years, rank), f32),
            pltpu.VMEM((depth, rank), f32),
            pltpu.VMEM((rank, depth), jnp.bfloat16),
            pltpu.VMEM((rank, rank), f32),
            pltpu.VMEM((2 * steps, rank, width), f32),
            pltpu.VMEM((2 * steps, rank, width), f32),
            pltpu.VMEM((steps, rank, width), f32),
            pltpu.VMEM((steps, rank, width), f32),
            pltpu.VMEM((steps, rank, width), f32),
            pltpu.VMEM((2, rank // 2, rank), f32),
            pltpu.VMEM((rank // 2, rank), f32),
            pltpu.VMEM((4, rank // 2, rank), f32),
            pltpu.VMEM((grid_sizes[0], rank // 2, rank), f32),
            pltpu.VMEM((grid_sizes[1], rank // 2, rank), f32),
            pltpu.VMEM((2, rank // 2, rank), f32),
            pltpu.SemaphoreType.DMA((4 * steps,)),
            pltpu.SemaphoreType.DMA((3,)),
            pltpu.SemaphoreType.DMA((copies,)),
            pltpu.SemaphoreType.DMA((copies,)),
        ],
        compiler_params=pltpu.CompilerParams(
            collective_id=0, has_side_effects=True, vmem_limit_bytes=48 << 20
        ),
    )(*operands)
    cell_factor, column_scale, cell_gram = pl.pallas_call(
        functools.partial(finish_kernel, float(total_cells)),
        out_shape=(
            jax.ShapeDtypeStruct((local_cells, rank), f32),
            jax.ShapeDtypeStruct((1, rank), f32),
            jax.ShapeDtypeStruct((rank, rank), f32),
        ),
        in_specs=[vmem, vmem],
        out_specs=(hbm, hbm, hbm),
        scratch_shapes=[
            pltpu.VMEM((local_cells, rank), f32),
            pltpu.VMEM((1, rank), f32),
            pltpu.VMEM((rank, rank), f32),
            pltpu.SemaphoreType.DMA((10,)),
        ],
        compiler_params=pltpu.CompilerParams(vmem_limit_bytes=16 << 20),
    )(raw, products)
    return cell_factor, column_scale.reshape(rank), cell_gram


def solution(mesh):
    cells = mesh.shape["cell"]
    grid_sizes = (4, cells // 8)
    in_specs = (P(None, "scen", None, "cell"), P(), P("scen", None), P())
    out_specs = (P("cell", None), P(), P())
    return jax.shard_map(
        functools.partial(on_device, grid_sizes), mesh=mesh, in_specs=in_specs, out_specs=out_specs, check_vma=False
    )
```

```python
import functools

import jax
import jax.numpy as jnp
from jax import lax
from jax.experimental import pallas as pl
from jax.experimental.pallas import tpu as pltpu
from jax.sharding import PartitionSpec as P

ridge = 0.1
epsilon = 1e-06
MESH = pl.DeviceIdType.MESH
HIGHEST = lax.Precision.HIGHEST
NT = (((1,), (1,)), ((), ()))
RANK = 128
PARTS = 4
PANEL = 16
WIDTHS = (128, 384, 384, 128)


def invert(normal, stage):
    rows = lax.broadcasted_iota(jnp.int32, (RANK, RANK), 0)
    cols = lax.broadcasted_iota(jnp.int32, (RANK, RANK), 1)
    panel_row = lax.broadcasted_iota(jnp.int32, (PANEL, RANK), 0)
    panel_col = lax.broadcasted_iota(jnp.int32, (PANEL, RANK), 1)
    a = normal
    for first in range(0, RANK, PANEL):
        panel = a[first : first + PANEL, :]
        columns = [
            jnp.broadcast_to(panel[:, first + j : first + j + 1], (PANEL, RANK))
            for j in range(PANEL)
        ]
        inside = (panel_col >= first) & (panel_col < first + PANEL)
        unit = jnp.where(panel_col - first == panel_row, 1.0, 0.0)
        right = jnp.where(inside, unit, panel)
        for k in range(PANEL):
            pivot = columns[k]
            scale = 1.0 / pivot[k : k + 1, :]
            is_pivot = panel_row == k
            top = right[k : k + 1, :] * scale
            right = jnp.where(is_pivot, top, right - pivot * top)
            for j in range(k + 1, PANEL):
                top = columns[j][k : k + 1, :] * scale
                columns[j] = jnp.where(is_pivot, top, columns[j] - pivot * top)
        parts = [right]
        if first:
            parts = [jnp.zeros((first, RANK), jnp.float32)] + parts
        if first + PANEL < RANK:
            parts = parts + [jnp.zeros((RANK - first - PANEL, RANK), jnp.float32)]
        spread = jnp.concatenate(parts, axis=0)
        in_cols = (cols >= first) & (cols < first + PANEL)
        in_rows = (rows >= first) & (rows < first + PANEL)
        update = jnp.dot(
            jnp.where(in_cols, a, 0.0), spread, precision=HIGHEST, preferred_element_type=jnp.float32
        )
        a = jnp.where(in_rows, spread, jnp.where(in_cols, 0.0, a) - update)
    return a


def gram(factor_ref, pad_ref):
    pad_ref[...] = jnp.zeros_like(pad_ref)
    pad_ref[0 : factor_ref.shape[0], :] = factor_ref[...]
    full = pad_ref[...]
    return jnp.dot(full.T, full, precision=HIGHEST, preferred_element_type=jnp.float32)


def turn(block, lanes):
    return jnp.concatenate([block[:, RANK - lanes :], block[:, : RANK - lanes]], axis=1)


def pack(whole, packed):
    lane = lax.broadcasted_iota(jnp.int32, (32, RANK), 1)
    packed[0, 0:32, :] = whole[0:32, :]
    packed[1, 0:32, :] = jnp.where(lane < 32, turn(whole[96:128, :], 32), whole[32:64, :])
    rest = jnp.where(lane[0:16] < 64, turn(whole[80:96, :], 64), whole[64:80, :])
    packed[0, 32:40, :] = rest[0:8, :]
    packed[1, 32:40, :] = rest[8:16, :]


def unpack(packed):
    rest = jnp.concatenate([packed[0, 32:40, :], packed[1, 32:40, :]], axis=0)
    second = packed[1, 0:32, :]
    upper = jnp.concatenate(
        [packed[0, 0:32, :], second, rest, turn(rest, 64), turn(second, 96)], axis=0
    )
    rows = jnp.right_shift(lax.broadcasted_iota(jnp.int32, (RANK, RANK), 0), 5)
    cols = jnp.right_shift(lax.broadcasted_iota(jnp.int32, (RANK, RANK), 1), 5)
    return jnp.where(cols >= rows, upper, upper.T)


def main_kernel(
    grid_sizes, widths, yields, model, scen, year, raw, g_out,
    ybufs, mbuf, sbuf, yearbuf, khat, kht, pad, csend, crecv, ysend, yrecv, own,
    gd, gcr, gy, gz, gx, gfin,
    yield_sems, factor_sems, send_sems, recv_sems,
):
    nz, nx = grid_sizes
    s = lax.axis_index("scen")
    c = lax.axis_index("cell")
    core = s % 2
    ylo = s // 2
    yhi = c % 2
    y = yhi * 2 + ylo
    x = (c // 2) % nx
    z = c // (2 * nx)
    quarter = yields.shape[1] // PARTS
    steps = len(widths)
    offsets = [sum(widths[:j]) for j in range(steps)]

    def device(core, y, z, x):
        return ((y % 2) * 2 + core, (z * nx + x) * 2 + y // 2)

    partner = device(1 - core, y, z, x)
    across = ((1 - ylo) * 2 + core, c)
    diagonal = ((1 - ylo) * 2 + 1 - core, c)
    y_peers = [device(core, (y + k) % 4, z, x) for k in (2, 1, 3)]
    z_peers = [device(core, y, (z + k) % nz, x) for k in (2, 1, 3)]
    x_peers = [device(core, y, z, (x + k) % nx) for k in (2, 1, 3)]
    first_slot = z * (1 - core) + x * core
    second_slot = x * (1 - core) + z * core
    first_peers = [
        device(core, y, (z + k * (1 - core)) % nz, (x + k * core) % nx) for k in (2, 1, 3)
    ]
    second_peers = [
        device(core, y, (z + k * core) % nz, (x + k * (1 - core)) % nx) for k in (2, 1, 3)
    ]

    sent = []
    received = set()

    def send(src, dst, target):
        n = len(sent)
        copy = pltpu.make_async_remote_copy(
            src_ref=src, dst_ref=dst, send_sem=send_sems.at[n], recv_sem=recv_sems.at[n],
            device_id=target, device_id_type=MESH,
        )
        copy.start()
        sent.append(copy)
        return n

    left = set()

    def leave(n):
        left.add(n)
        sent[n].wait_send()

    def arrive(n):
        received.add(n)
        sent[n].wait_recv()

    q_across = (1 - ylo) * 2 + core
    q_diagonal = (1 - ylo) * 2 + 1 - core
    q_partner = ylo * 2 + 1 - core
    order = []
    for first, second in ((q_diagonal, q_across), (q_partner, s)):
        for j in range(steps):
            order += [(first, j), (second, j)]

    factor_copies = [
        pltpu.make_async_copy(src, dst, factor_sems.at[i])
        for i, (src, dst) in enumerate(((model, mbuf), (scen, sbuf.at[s]), (year, yearbuf)))
    ]
    for copy in factor_copies:
        copy.start()

    def columns(q, j):
        return pl.ds(pl.multiple_of(q * quarter + offsets[j], 128), widths[j])

    loads = []
    for i, (q, j) in enumerate(order):
        slot = ybufs.at[i, :, pl.ds(0, widths[j])]
        loads.append(pltpu.make_async_copy(yields.at[:, columns(q, j)], slot, yield_sems.at[i]))
    ahead = [0]

    def load_until(n):
        for copy in loads[ahead[0] : n]:
            copy.start()
        ahead[0] = max(ahead[0], min(n, len(loads)))

    load_until(2)
    barrier = pltpu.get_barrier_semaphore()
    peers = [partner, diagonal] + y_peers + z_peers + x_peers
    for peer in peers:
        pl.semaphore_signal(barrier, inc=1, device_id=peer, device_id_type=MESH)

    for copy in factor_copies:
        copy.wait()
    local_scen = sbuf[s]
    years = yearbuf.shape[0]
    block = 8 * years
    for m in range(mbuf.shape[0]):
        ms = mbuf[m : m + 1, :] * local_scen
        khat[m * block : (m + 1) * block, :] = (ms[None, :, :] * yearbuf[...][:, None, :]).reshape(
            block, RANK
        )
    depth = khat.shape[0]
    for first in range(0, depth, RANK):
        size = min(RANK, depth - first)
        kht[:, first : first + size] = khat[first : first + size, :].T.astype(jnp.bfloat16)

    def product(i):
        loads[i].wait()
        load_until(i + 6)
        return jnp.dot(
            kht[...], ybufs[i, :, 0 : widths[order[i][1]]], preferred_element_type=jnp.float32
        )

    def part(ref, n):
        return ref.at[n, :, pl.ds(0, widths[n % steps])]

    part(csend, 0)[...] = product(0)
    pl.semaphore_wait(barrier, len(peers))
    to_partner = [send(part(csend, 0), part(crecv, 0), partner)]
    scen_copies = []
    crossings = []
    gathers = []
    late = []

    def rows_of(q, j):
        return pl.ds(pl.multiple_of(q * quarter + offsets[j], 128), widths[j])

    for j in range(steps):
        part(ysend, j)[...] = product(2 * j + 1)
        n = j + 1
        if j:
            part(csend, n)[...] = product(2 * n)
            to_partner.append(send(part(csend, n), part(crecv, n), partner))
        arrive(to_partner[j])
        part(ysend, j)[...] = part(ysend, j)[...] + part(crecv, j)[...]
        crossings.append(send(part(ysend, j), part(yrecv, j), across))
        if j == 0:
            scen_copies = [
                send(sbuf.at[s], sbuf.at[s], peer) for peer in (across, diagonal, partner)
            ]
            part(csend, n)[...] = product(2 * n)
            to_partner.append(send(part(csend, n), part(crecv, n), partner))
    for j in range(steps):
        n = steps + j
        part(own, j)[...] = product(2 * n + 1)
        if j + 1 < steps:
            part(csend, n + 1)[...] = product(2 * n + 2)
            to_partner.append(send(part(csend, n + 1), part(crecv, n + 1), partner))

    for n in scen_copies:
        arrive(n)
    gram_model = gram(mbuf, pad)
    gram_year = gram(yearbuf, pad)
    whole_scen = sbuf[...].reshape(PARTS * sbuf.shape[1], RANK)
    pad[...] = jnp.zeros_like(pad)
    pad[0 : PARTS * sbuf.shape[1], :] = whole_scen
    full = pad[...]
    gram_scen = jnp.dot(full.T, full, precision=HIGHEST, preferred_element_type=jnp.float32)
    rows = lax.broadcasted_iota(jnp.int32, (RANK, RANK), 0)
    cols = lax.broadcasted_iota(jnp.int32, (RANK, RANK), 1)
    normal = gram_model * gram_scen * gram_year + jnp.where(rows == cols, ridge, 0.0)
    inverse = invert(normal, pad)

    total = jnp.zeros((RANK, RANK), jnp.float32)

    def keep(j, solved):
        raw[rows_of(s, j), :] = solved.T
        here = raw.at[rows_of(s, j)]
        gathers.append(send(here, here, across))
        late.append(send(here, here, partner))

    for j in range(steps):
        arrive(to_partner[steps + j])
        arrive(crossings[j])
        summed = part(own, j)[...] + part(crecv, steps + j)[...] + part(yrecv, j)[...]
        solved = jnp.dot(inverse, summed, precision=HIGHEST, preferred_element_type=jnp.float32)
        total = total + lax.dot_general(
            solved, solved, NT, precision=HIGHEST, preferred_element_type=jnp.float32
        )
        if j + 1 < steps:
            keep(j, solved)

    pack(total, gd)
    halves = send(gd.at[1 - core], gcr, partner)
    keep(steps - 1, solved)
    arrive(halves)
    value = gd[core] + gcr[...]
    for phase, (where, slots, targets) in enumerate(
        ((first_slot, gz, first_peers), (second_slot, gx, second_peers), (y, gy, y_peers))
    ):
        slots[where] = value
        done = list(sent)
        copies = [send(slots.at[where], slots.at[where], target) for target in targets]
        if phase == 2:
            for j in range(steps):
                arrive(gathers[j])
                here = raw.at[rows_of(q_across, j)]
                late.append(send(here, here, partner))
        for n, copy in enumerate(done):
            if n not in left and (phase == 2 or n not in gathers):
                leave(n)
        for n in copies:
            arrive(n)
        value = slots[0]
        for k in range(1, slots.shape[0]):
            value = value + slots[k]
    gfin[core] = value
    last = send(gfin.at[core], gfin.at[core], partner)
    for n in range(len(sent)):
        if n != last:
            if n not in left:
                leave(n)
            if n not in received:
                arrive(n)
    arrive(last)
    g_out[...] = unpack(gfin)
    leave(last)


def finish_kernel(cells, raw, g, factor, scale, cell_gram, scaled, small, grams, sems):
    rows = lax.broadcasted_iota(jnp.int32, (RANK, RANK), 0)
    cols = lax.broadcasted_iota(jnp.int32, (RANK, RANK), 1)
    products = g[...]
    diagonal = jnp.where(rows == cols, products, 0.0)
    along = jnp.sqrt(jnp.sum(diagonal, axis=0, keepdims=True) / cells + epsilon)
    inverse = 1.0 / along
    copies = []
    count = sems.shape[0] - 2
    rows_each = raw.shape[0] // count
    for i in range(count):
        here = pl.ds(i * rows_each, rows_each)
        scaled[here, :] = raw[here, :] * inverse
        copies.append(pltpu.make_async_copy(scaled.at[here], factor.at[here], sems.at[i]))
        copies[-1].start()
    down = jnp.sqrt(jnp.sum(diagonal, axis=1, keepdims=True) / cells + epsilon)
    small[...] = along
    grams[...] = products * inverse * (1.0 / down) / cells
    copies.append(pltpu.make_async_copy(small, scale, sems.at[count]))
    copies.append(pltpu.make_async_copy(grams, cell_gram, sems.at[count + 1]))
    copies[-1].start()
    copies[-2].start()
    for copy in copies:
        copy.wait()


def on_device(grid_sizes, yields, model_factor, scen_factor, year_factor):
    models, scens, years, local_cells = yields.shape
    rank = model_factor.shape[1]
    total_cells = local_cells * lax.axis_size("cell")
    flat = yields.transpose(0, 2, 1, 3).reshape(-1, local_cells)
    depth = flat.shape[0]
    steps = len(WIDTHS)
    width = max(WIDTHS)
    f32 = jnp.float32
    hbm = pl.BlockSpec(memory_space=pltpu.HBM)
    vmem = pl.BlockSpec(memory_space=pltpu.VMEM)
    copies = 64
    operands = [
        pltpu.with_memory_space_constraint(array, pltpu.HBM)
        for array in (flat, model_factor, scen_factor, year_factor)
    ]
    raw, products = pl.pallas_call(
        functools.partial(main_kernel, grid_sizes, WIDTHS),
        out_shape=(
            pltpu.VMEM((local_cells, rank), f32),
            pltpu.VMEM((rank, rank), f32),
        ),
        in_specs=[hbm] * 4,
        out_specs=(vmem, vmem),
        scratch_shapes=[
            pltpu.VMEM((4 * steps, depth, width), jnp.bfloat16),
            pltpu.VMEM((models, rank), f32),
            pltpu.VMEM((PARTS, scens, rank), f32),
            pltpu.VMEM((years, rank), f32),
            pltpu.VMEM((depth, rank), f32),
            pltpu.VMEM((rank, depth), jnp.bfloat16),
            pltpu.VMEM((rank, rank), f32),
            pltpu.VMEM((2 * steps, rank, width), f32),
            pltpu.VMEM((2 * steps, rank, width), f32),
            pltpu.VMEM((steps, rank, width), f32),
            pltpu.VMEM((steps, rank, width), f32),
            pltpu.VMEM((steps, rank, width), f32),
            pltpu.VMEM((2, 40, rank), f32),
            pltpu.VMEM((40, rank), f32),
            pltpu.VMEM((4, 40, rank), f32),
            pltpu.VMEM((grid_sizes[0], 40, rank), f32),
            pltpu.VMEM((grid_sizes[1], 40, rank), f32),
            pltpu.VMEM((2, 40, rank), f32),
            pltpu.SemaphoreType.DMA((4 * steps,)),
            pltpu.SemaphoreType.DMA((3,)),
            pltpu.SemaphoreType.DMA((copies,)),
            pltpu.SemaphoreType.DMA((copies,)),
        ],
        compiler_params=pltpu.CompilerParams(
            collective_id=0, has_side_effects=True, vmem_limit_bytes=48 << 20
        ),
    )(*operands)
    cell_factor, column_scale, cell_gram = pl.pallas_call(
        functools.partial(finish_kernel, float(total_cells)),
        out_shape=(
            jax.ShapeDtypeStruct((local_cells, rank), f32),
            jax.ShapeDtypeStruct((1, rank), f32),
            jax.ShapeDtypeStruct((rank, rank), f32),
        ),
        in_specs=[vmem, vmem],
        out_specs=(hbm, hbm, hbm),
        scratch_shapes=[
            pltpu.VMEM((local_cells, rank), f32),
            pltpu.VMEM((1, rank), f32),
            pltpu.VMEM((rank, rank), f32),
            pltpu.SemaphoreType.DMA((10,)),
        ],
        compiler_params=pltpu.CompilerParams(vmem_limit_bytes=16 << 20),
    )(raw, products)
    return cell_factor, column_scale.reshape(rank), cell_gram


def solution(mesh):
    cells = mesh.shape["cell"]
    grid_sizes = (4, cells // 8)
    in_specs = (P(None, "scen", None, "cell"), P(), P("scen", None), P())
    out_specs = (P("cell", None), P(), P())
    return jax.shard_map(
        functools.partial(on_device, grid_sizes), mesh=mesh, in_specs=in_specs, out_specs=out_specs, check_vma=False
    )
```

```python
import functools

import jax
import jax.numpy as jnp
from jax import lax
from jax.experimental import pallas as pl
from jax.experimental.pallas import tpu as pltpu
from jax.sharding import PartitionSpec as P

ridge = 0.1
epsilon = 1e-06
MESH = pl.DeviceIdType.MESH
HIGHEST = lax.Precision.HIGHEST
NT = (((1,), (1,)), ((), ()))
RANK = 128
PARTS = 4
PANEL = 16
WIDTHS = (128, 256, 384, 256)


def invert(normal, stage):
    rows = lax.broadcasted_iota(jnp.int32, (RANK, RANK), 0)
    cols = lax.broadcasted_iota(jnp.int32, (RANK, RANK), 1)
    panel_row = lax.broadcasted_iota(jnp.int32, (PANEL, RANK), 0)
    panel_col = lax.broadcasted_iota(jnp.int32, (PANEL, RANK), 1)
    a = normal
    for first in range(0, RANK, PANEL):
        panel = a[first : first + PANEL, :]
        columns = [
            jnp.broadcast_to(panel[:, first + j : first + j + 1], (PANEL, RANK))
            for j in range(PANEL)
        ]
        inside = (panel_col >= first) & (panel_col < first + PANEL)
        unit = jnp.where(panel_col - first == panel_row, 1.0, 0.0)
        right = jnp.where(inside, unit, panel)
        for k in range(PANEL):
            pivot = columns[k]
            scale = 1.0 / pivot[k : k + 1, :]
            is_pivot = panel_row == k
            top = right[k : k + 1, :] * scale
            right = jnp.where(is_pivot, top, right - pivot * top)
            for j in range(k + 1, PANEL):
                top = columns[j][k : k + 1, :] * scale
                columns[j] = jnp.where(is_pivot, top, columns[j] - pivot * top)
        parts = [right]
        if first:
            parts = [jnp.zeros((first, RANK), jnp.float32)] + parts
        if first + PANEL < RANK:
            parts = parts + [jnp.zeros((RANK - first - PANEL, RANK), jnp.float32)]
        spread = jnp.concatenate(parts, axis=0)
        in_cols = (cols >= first) & (cols < first + PANEL)
        in_rows = (rows >= first) & (rows < first + PANEL)
        update = jnp.dot(
            jnp.where(in_cols, a, 0.0), spread, precision=HIGHEST, preferred_element_type=jnp.float32
        )
        a = jnp.where(in_rows, spread, jnp.where(in_cols, 0.0, a) - update)
    return a


def gram(factor_ref, pad_ref):
    pad_ref[...] = jnp.zeros_like(pad_ref)
    pad_ref[0 : factor_ref.shape[0], :] = factor_ref[...]
    full = pad_ref[...]
    return jnp.dot(full.T, full, precision=HIGHEST, preferred_element_type=jnp.float32)


def turn(block, lanes):
    return jnp.concatenate([block[:, RANK - lanes :], block[:, : RANK - lanes]], axis=1)


def pack(whole, packed):
    lane = lax.broadcasted_iota(jnp.int32, (32, RANK), 1)
    packed[0, 0:32, :] = whole[0:32, :]
    packed[1, 0:32, :] = jnp.where(lane < 32, turn(whole[96:128, :], 32), whole[32:64, :])
    rest = jnp.where(lane[0:16] < 64, turn(whole[80:96, :], 64), whole[64:80, :])
    packed[0, 32:40, :] = rest[0:8, :]
    packed[1, 32:40, :] = rest[8:16, :]


def unpack(packed):
    rest = jnp.concatenate([packed[0, 32:40, :], packed[1, 32:40, :]], axis=0)
    second = packed[1, 0:32, :]
    upper = jnp.concatenate(
        [packed[0, 0:32, :], second, rest, turn(rest, 64), turn(second, 96)], axis=0
    )
    rows = jnp.right_shift(lax.broadcasted_iota(jnp.int32, (RANK, RANK), 0), 5)
    cols = jnp.right_shift(lax.broadcasted_iota(jnp.int32, (RANK, RANK), 1), 5)
    return jnp.where(cols >= rows, upper, upper.T)


def main_kernel(
    grid_sizes, widths, yields, model, scen, year, raw, g_out,
    ybufs, mbuf, sbuf, yearbuf, khat, kht, pad, csend, crecv, ysend, yrecv, own,
    gd, gcr, gy, gz, gx, gfin,
    yield_sems, factor_sems, send_sems, recv_sems,
):
    nz, nx = grid_sizes
    s = lax.axis_index("scen")
    c = lax.axis_index("cell")
    core = s % 2
    ylo = s // 2
    yhi = c % 2
    y = yhi * 2 + ylo
    x = (c // 2) % nx
    z = c // (2 * nx)
    quarter = yields.shape[1] // PARTS
    steps = len(widths)
    offsets = [sum(widths[:j]) for j in range(steps)]

    def device(core, y, z, x):
        return ((y % 2) * 2 + core, (z * nx + x) * 2 + y // 2)

    partner = device(1 - core, y, z, x)
    across = ((1 - ylo) * 2 + core, c)
    diagonal = ((1 - ylo) * 2 + 1 - core, c)
    y_peers = [device(core, (y + k) % 4, z, x) for k in (2, 1, 3)]
    z_peers = [device(core, y, (z + k) % nz, x) for k in (2, 1, 3)]
    x_peers = [device(core, y, z, (x + k) % nx) for k in (2, 1, 3)]
    first_slot = z * (1 - core) + x * core
    second_slot = x * (1 - core) + z * core
    first_peers = [
        device(core, y, (z + k * (1 - core)) % nz, (x + k * core) % nx) for k in (2, 1, 3)
    ]
    second_peers = [
        device(core, y, (z + k * core) % nz, (x + k * (1 - core)) % nx) for k in (2, 1, 3)
    ]

    sent = []
    received = set()

    def send(src, dst, target):
        n = len(sent)
        copy = pltpu.make_async_remote_copy(
            src_ref=src, dst_ref=dst, send_sem=send_sems.at[n], recv_sem=recv_sems.at[n],
            device_id=target, device_id_type=MESH,
        )
        copy.start()
        sent.append(copy)
        return n

    left = set()

    def leave(n):
        left.add(n)
        sent[n].wait_send()

    def arrive(n):
        received.add(n)
        sent[n].wait_recv()

    q_across = (1 - ylo) * 2 + core
    q_diagonal = (1 - ylo) * 2 + 1 - core
    q_partner = ylo * 2 + 1 - core
    order = []
    for first, second in ((q_diagonal, q_across), (q_partner, s)):
        for j in range(steps):
            order += [(first, j), (second, j)]

    factor_copies = [
        pltpu.make_async_copy(src, dst, factor_sems.at[i])
        for i, (src, dst) in enumerate(((model, mbuf), (scen, sbuf.at[s]), (year, yearbuf)))
    ]
    for copy in factor_copies:
        copy.start()

    def columns(q, j):
        return pl.ds(pl.multiple_of(q * quarter + offsets[j], 128), widths[j])

    loads = []
    for i, (q, j) in enumerate(order):
        slot = ybufs.at[i, :, pl.ds(0, widths[j])]
        loads.append(pltpu.make_async_copy(yields.at[:, columns(q, j)], slot, yield_sems.at[i]))
    ahead = [0]

    def load_until(n):
        for copy in loads[ahead[0] : n]:
            copy.start()
        ahead[0] = max(ahead[0], min(n, len(loads)))

    load_until(2)
    barrier = pltpu.get_barrier_semaphore()
    peers = [partner, diagonal] + y_peers + z_peers + x_peers
    for peer in peers:
        pl.semaphore_signal(barrier, inc=1, device_id=peer, device_id_type=MESH)

    for copy in factor_copies:
        copy.wait()
    local_scen = sbuf[s]
    years = yearbuf.shape[0]
    block = 8 * years
    for m in range(mbuf.shape[0]):
        ms = mbuf[m : m + 1, :] * local_scen
        khat[m * block : (m + 1) * block, :] = (ms[None, :, :] * yearbuf[...][:, None, :]).reshape(
            block, RANK
        )
    depth = khat.shape[0]
    for first in range(0, depth, RANK):
        size = min(RANK, depth - first)
        kht[:, first : first + size] = khat[first : first + size, :].T.astype(jnp.bfloat16)

    def product(i):
        loads[i].wait()
        load_until(i + 6)
        return jnp.dot(
            kht[...], ybufs[i, :, 0 : widths[order[i][1]]], preferred_element_type=jnp.float32
        )

    def part(ref, n):
        return ref.at[n, :, pl.ds(0, widths[n % steps])]

    part(csend, 0)[...] = product(0)
    pl.semaphore_wait(barrier, len(peers))
    to_partner = [send(part(csend, 0), part(crecv, 0), partner)]
    scen_copies = []
    crossings = []
    gathers = []
    late = []

    def rows_of(q, j):
        return pl.ds(pl.multiple_of(q * quarter + offsets[j], 128), widths[j])

    for j in range(steps):
        part(ysend, j)[...] = product(2 * j + 1)
        n = j + 1
        if j:
            part(csend, n)[...] = product(2 * n)
            to_partner.append(send(part(csend, n), part(crecv, n), partner))
        arrive(to_partner[j])
        part(ysend, j)[...] = part(ysend, j)[...] + part(crecv, j)[...]
        crossings.append(send(part(ysend, j), part(yrecv, j), across))
        if j == 0:
            scen_copies = [
                send(sbuf.at[s], sbuf.at[s], peer) for peer in (across, diagonal, partner)
            ]
            part(csend, n)[...] = product(2 * n)
            to_partner.append(send(part(csend, n), part(crecv, n), partner))
    for j in range(steps):
        n = steps + j
        part(own, j)[...] = product(2 * n + 1)
        if j + 1 < steps:
            part(csend, n + 1)[...] = product(2 * n + 2)
            to_partner.append(send(part(csend, n + 1), part(crecv, n + 1), partner))

    for n in scen_copies:
        arrive(n)
    gram_model = gram(mbuf, pad)
    gram_year = gram(yearbuf, pad)
    whole_scen = sbuf[...].reshape(PARTS * sbuf.shape[1], RANK)
    pad[...] = jnp.zeros_like(pad)
    pad[0 : PARTS * sbuf.shape[1], :] = whole_scen
    full = pad[...]
    gram_scen = jnp.dot(full.T, full, precision=HIGHEST, preferred_element_type=jnp.float32)
    rows = lax.broadcasted_iota(jnp.int32, (RANK, RANK), 0)
    cols = lax.broadcasted_iota(jnp.int32, (RANK, RANK), 1)
    normal = gram_model * gram_scen * gram_year + jnp.where(rows == cols, ridge, 0.0)
    inverse = invert(normal, pad)

    total = jnp.zeros((RANK, RANK), jnp.float32)

    def keep(j, solved):
        raw[rows_of(s, j), :] = solved.T
        here = raw.at[rows_of(s, j)]
        gathers.append(send(here, here, across))
        late.append(send(here, here, partner))

    for j in range(steps):
        arrive(to_partner[steps + j])
        arrive(crossings[j])
        summed = part(own, j)[...] + part(crecv, steps + j)[...] + part(yrecv, j)[...]
        solved = jnp.dot(inverse, summed, precision=HIGHEST, preferred_element_type=jnp.float32)
        total = total + lax.dot_general(
            solved, solved, NT, precision=HIGHEST, preferred_element_type=jnp.float32
        )
        if j + 1 < steps:
            keep(j, solved)

    pack(total, gd)
    halves = send(gd.at[1 - core], gcr, partner)
    keep(steps - 1, solved)
    arrive(halves)
    value = gd[core] + gcr[...]
    for phase, (where, slots, targets) in enumerate(
        ((first_slot, gz, first_peers), (second_slot, gx, second_peers), (y, gy, y_peers))
    ):
        slots[where] = value
        done = list(sent)
        copies = [send(slots.at[where], slots.at[where], target) for target in targets]
        if phase == 2:
            for j in range(steps):
                arrive(gathers[j])
                here = raw.at[rows_of(q_across, j)]
                late.append(send(here, here, partner))
        for n, copy in enumerate(done):
            if n not in left and (phase == 2 or n not in gathers):
                leave(n)
        for n in copies:
            arrive(n)
        value = slots[0]
        for k in range(1, slots.shape[0]):
            value = value + slots[k]
    gfin[core] = value
    last = send(gfin.at[core], gfin.at[core], partner)
    for n in range(len(sent)):
        if n != last:
            if n not in left:
                leave(n)
            if n not in received:
                arrive(n)
    arrive(last)
    g_out[...] = unpack(gfin)
    leave(last)


def finish_kernel(cells, raw, g, factor, scale, cell_gram, scaled, small, grams, sems):
    rows = lax.broadcasted_iota(jnp.int32, (RANK, RANK), 0)
    cols = lax.broadcasted_iota(jnp.int32, (RANK, RANK), 1)
    products = g[...]
    diagonal = jnp.where(rows == cols, products, 0.0)
    along = jnp.sqrt(jnp.sum(diagonal, axis=0, keepdims=True) / cells + epsilon)
    inverse = 1.0 / along
    copies = []
    count = sems.shape[0] - 2
    rows_each = raw.shape[0] // count
    for i in range(count):
        here = pl.ds(i * rows_each, rows_each)
        scaled[here, :] = raw[here, :] * inverse
        copies.append(pltpu.make_async_copy(scaled.at[here], factor.at[here], sems.at[i]))
        copies[-1].start()
    down = jnp.sqrt(jnp.sum(diagonal, axis=1, keepdims=True) / cells + epsilon)
    small[...] = along
    grams[...] = products * inverse * (1.0 / down) / cells
    copies.append(pltpu.make_async_copy(small, scale, sems.at[count]))
    copies.append(pltpu.make_async_copy(grams, cell_gram, sems.at[count + 1]))
    copies[-1].start()
    copies[-2].start()
    for copy in copies:
        copy.wait()


def on_device(grid_sizes, yields, model_factor, scen_factor, year_factor):
    models, scens, years, local_cells = yields.shape
    rank = model_factor.shape[1]
    total_cells = local_cells * lax.axis_size("cell")
    flat = yields.transpose(0, 2, 1, 3).reshape(-1, local_cells)
    depth = flat.shape[0]
    steps = len(WIDTHS)
    width = max(WIDTHS)
    f32 = jnp.float32
    hbm = pl.BlockSpec(memory_space=pltpu.HBM)
    vmem = pl.BlockSpec(memory_space=pltpu.VMEM)
    copies = 64
    operands = [
        pltpu.with_memory_space_constraint(array, pltpu.HBM)
        for array in (flat, model_factor, scen_factor, year_factor)
    ]
    raw, products = pl.pallas_call(
        functools.partial(main_kernel, grid_sizes, WIDTHS),
        out_shape=(
            pltpu.VMEM((local_cells, rank), f32),
            pltpu.VMEM((rank, rank), f32),
        ),
        in_specs=[hbm] * 4,
        out_specs=(vmem, vmem),
        scratch_shapes=[
            pltpu.VMEM((4 * steps, depth, width), jnp.bfloat16),
            pltpu.VMEM((models, rank), f32),
            pltpu.VMEM((PARTS, scens, rank), f32),
            pltpu.VMEM((years, rank), f32),
            pltpu.VMEM((depth, rank), f32),
            pltpu.VMEM((rank, depth), jnp.bfloat16),
            pltpu.VMEM((rank, rank), f32),
            pltpu.VMEM((2 * steps, rank, width), f32),
            pltpu.VMEM((2 * steps, rank, width), f32),
            pltpu.VMEM((steps, rank, width), f32),
            pltpu.VMEM((steps, rank, width), f32),
            pltpu.VMEM((steps, rank, width), f32),
            pltpu.VMEM((2, 40, rank), f32),
            pltpu.VMEM((40, rank), f32),
            pltpu.VMEM((4, 40, rank), f32),
            pltpu.VMEM((grid_sizes[0], 40, rank), f32),
            pltpu.VMEM((grid_sizes[1], 40, rank), f32),
            pltpu.VMEM((2, 40, rank), f32),
            pltpu.SemaphoreType.DMA((4 * steps,)),
            pltpu.SemaphoreType.DMA((3,)),
            pltpu.SemaphoreType.DMA((copies,)),
            pltpu.SemaphoreType.DMA((copies,)),
        ],
        compiler_params=pltpu.CompilerParams(
            collective_id=0, has_side_effects=True, vmem_limit_bytes=48 << 20
        ),
    )(*operands)
    cell_factor, column_scale, cell_gram = pl.pallas_call(
        functools.partial(finish_kernel, float(total_cells)),
        out_shape=(
            jax.ShapeDtypeStruct((local_cells, rank), f32),
            jax.ShapeDtypeStruct((1, rank), f32),
            jax.ShapeDtypeStruct((rank, rank), f32),
        ),
        in_specs=[vmem, vmem],
        out_specs=(hbm, hbm, hbm),
        scratch_shapes=[
            pltpu.VMEM((local_cells, rank), f32),
            pltpu.VMEM((1, rank), f32),
            pltpu.VMEM((rank, rank), f32),
            pltpu.SemaphoreType.DMA((10,)),
        ],
        compiler_params=pltpu.CompilerParams(vmem_limit_bytes=16 << 20),
    )(raw, products)
    return cell_factor, column_scale.reshape(rank), cell_gram


def solution(mesh):
    cells = mesh.shape["cell"]
    grid_sizes = (4, cells // 8)
    in_specs = (P(None, "scen", None, "cell"), P(), P("scen", None), P())
    out_specs = (P("cell", None), P(), P())
    return jax.shard_map(
        functools.partial(on_device, grid_sizes), mesh=mesh, in_specs=in_specs, out_specs=out_specs, check_vma=False
    )
```
